32 devices in a mesh: groups: 2 (over y), blk: 16 (over z, x, core).
Axes of the slice: x: 2, y: 2, z: 4, core: 2. Of those that a mesh axis runs over, the one named last changes fastest.
Arguments:
- snapshots: bfloat16 [64, 64, 16, 128], P(None, ('groups', 'blk')), parts along dimension 1, may hold values from -200 to 200
- old_modes: bfloat16 [192, 64, 16, 128], P(None, ('groups', 'blk')), parts along dimension 1, may hold values from -60 to 60
- mode_scales: float32 [384], P('groups'), parts along dimension 0, may hold values from 0.3 to 3
- plane_counts: int32 [32], P(('groups', 'blk')), parts along dimension 0, may hold values from 1 to 2, 20 in all
- links: int32 [32, 2], P(('groups', 'blk')), parts along dimension 0, may hold values from 0 to 1, as said below
Outputs:
- new_modes: bfloat16 [256, 64, 16, 128], P(None, ('groups', 'blk')), parts along dimension 1
- factor: float32 [512, 256], P('groups'), parts along dimension 0
The draws below stay inside these ranges and needn't reach their ends.
There are 2 independent parts, one for each index of `groups`. The reference program is written for one: setup_inputs(seed, part) draws one part's arguments, and reference() takes and returns one part's arrays. A program takes and returns all parts, laid end to end along the dimension named above; each array names one. Nothing has to cross between parts.
Inputs may be any that keep to these rules, and one draw needn't show every extreme that they name: links[b, 1] equals links[b + 1 mod 16, 0]; 1 joins two blocks, 0 is a wall.
All inputs are finite; a program needn't handle non-finite values. No bound on the sum of `plane_counts` on one device may be relied on, other than what follows from the above.
Results may differ from the reference program's by a relative error of at most 0.0095.
Values may be sent and summed in bfloat16 or wider, within the bound.
A program may use at most 128 MiB of HBM per device.

```python
import math
import jax
import jax.numpy as jnp
import numpy as np
from jax import lax

NEW = 64
KEEP = 192
LMAX = 2
CY = 16
CZ = 128
COLS = 256
BLOCKS = 16
PLANES = 32
CELLS = 65536


def common_fields(key):
    base = jax.random.fold_in(key, 11)
    key_one, key_two, key_three = jax.random.split(base, 3)
    mode_noise = jnp.clip(jax.random.normal(key_one, (KEEP, PLANES, CY, CZ), jnp.float32), -4.0, 4.0)
    shared = jnp.clip(jax.random.normal(key_two, (PLANES, CY, CZ), jnp.float32), -4.0, 4.0)
    low_end, high_end = (0.3, 3.0)
    position = jnp.arange(PLANES, dtype=jnp.float32) / (PLANES - 1)
    plane_scale = jnp.exp(jax.random.uniform(key_three, (PLANES,), jnp.float32, jnp.log(low_end), jnp.log(high_end)))
    plane_scale = plane_scale * jnp.sqrt(1.0 + 2.0 * position)
    return (mode_noise, shared, plane_scale)


def draw_old_modes(key, part):
    mode_noise, shared, plane_scale = common_fields(key)
    values = (mode_noise + 0.5 * shared[None]) * plane_scale[None, :, None, None]
    return values.astype(jnp.bfloat16)


def draw_snapshots(key, part):
    mode_noise, shared, plane_scale = common_fields(key)
    own_key, column_key = jax.random.split(jax.random.fold_in(key, 23))
    noise = jnp.clip(jax.random.normal(own_key, (NEW, PLANES, CY, CZ), jnp.float32), -4.0, 4.0)
    column_scale = jnp.exp(jax.random.uniform(column_key, (NEW,), jnp.float32, jnp.log(0.3), jnp.log(3.0)))
    values = noise + 0.8 * mode_noise[:NEW] + 0.5 * shared[None]
    values = values * plane_scale[None, :, None, None] * column_scale[:, None, None, None]
    return values.astype(jnp.bfloat16)


def draw_links(key, part):
    joined = (jax.random.randint(jax.random.fold_in(key, 5), (BLOCKS,), 0, 4) != 0).astype(jnp.int32)
    return jnp.stack([jnp.roll(joined, 1), joined], axis=1)


def length_profile(amount, total, most, skew):
    weights = [(1 << 20) // math.isqrt(rank ** skew) + 1 for rank in range(2, amount + 1)]
    rest, holding = total - most - (amount - 1), [1] * (amount - 1)
    while rest > 0:
        movable = [i for i in range(amount - 1) if holding[i] < most]
        mass, remaining = sum([weights[i] for i in movable]), rest
        for i in movable:
            extra = min(most - holding[i], max(1, remaining * weights[i] // mass), rest)
            holding[i] = holding[i] + extra
            rest = rest - extra
    return np.array([most] + holding)


def uneven(stream_key, amount, total, limit, lean):
    if amount == 2:
        one = jax.random.randint(stream_key, (), max(1, total - limit), min(limit, total - 1) + 1)
        return jnp.stack([one, total - one])
    lengths = jnp.asarray(length_profile(amount, total, limit, lean), jnp.int32)
    pairs = (amount - 1) // 2
    donor, taker = lengths[1:1 + 2 * pairs:2], lengths[2:2 + 2 * pairs:2]
    room = jnp.minimum(donor - 1, limit - taker)
    shifted = jax.random.randint(jax.random.fold_in(stream_key, 1), (pairs,), 0, 1 << 20) % (room + 1)
    lengths = lengths.at[1:1 + 2 * pairs:2].set(donor - shifted).at[2:2 + 2 * pairs:2].set(taker + shifted)
    return lengths[jax.random.permutation(jax.random.fold_in(stream_key, 2), amount)]


def setup_inputs(seed: int = 0, part: int = 0) -> dict:
    seeds = jax.random.split(jax.random.key(seed), 6)
    own_keys = jax.random.split(jax.random.fold_in(seeds[5], part), 6)
    snapshots = draw_snapshots(jax.random.fold_in(jax.random.fold_in(seeds[5], part), 71), part)
    old_modes = draw_old_modes(jax.random.fold_in(jax.random.fold_in(seeds[5], part), 71), part)
    mode_scales = jnp.clip(jnp.exp(jax.random.uniform(own_keys[2], (KEEP,), jnp.float32, math.log(0.3), math.log(3.0))), 0.3, 3.0)
    plane_counts = uneven(own_keys[3], BLOCKS, BLOCKS * LMAX * 5 // 8, LMAX, 2).astype(jnp.int32)
    links = draw_links(jax.random.fold_in(jax.random.fold_in(seeds[5], part), 71), part)
    return dict(snapshots=snapshots, old_modes=old_modes, mode_scales=mode_scales, plane_counts=plane_counts, links=links)


def smooth_along(field, along):
    widths = [(0, 0)] * field.ndim
    widths[along] = (1, 1)
    padded = jnp.pad(field, widths)
    length = field.shape[along]
    lower = lax.slice_in_dim(padded, 0, length, axis=along)
    upper = lax.slice_in_dim(padded, 2, length + 2, axis=along)
    return 0.25 * lower + 0.5 * field + 0.25 * upper

def reference(snapshots, old_modes, mode_scales, plane_counts, links):
    shaped = snapshots.astype(jnp.float32).reshape(NEW, BLOCKS, LMAX, CY, CZ)
    plane_ids = jnp.arange(LMAX, dtype=jnp.int32)
    alive = (plane_ids[None, :] < plane_counts[:, None]).astype(jnp.float32)
    last_pick = (plane_ids[None, :] == plane_counts[:, None] - 1).astype(jnp.float32)
    masked = shaped * alive[None, :, :, None, None]
    last_plane = jnp.sum(masked * last_pick[None, :, :, None, None], axis=2)
    first_plane = masked[:, :, 0]
    left_halo = jnp.roll(last_plane, 1, axis=1) * links[:, 0].astype(jnp.float32)[None, :, None, None]
    right_halo = jnp.roll(first_plane, -1, axis=1) * links[:, 1].astype(jnp.float32)[None, :, None, None]
    behind = jnp.concatenate([left_halo[:, :, None], masked[:, :, :-1]], axis=2)
    forward = jnp.concatenate([masked[:, :, 1:], jnp.zeros_like(masked[:, :, :1])], axis=2)
    forward = forward + last_pick[None, :, :, None, None] * right_halo[:, :, None]
    along_planes = 0.25 * behind + 0.5 * masked + 0.25 * forward
    smoothed = smooth_along(smooth_along(along_planes, 3), 4)
    filtered = (smoothed * alive[None, :, :, None, None]).astype(jnp.bfloat16)
    filtered = filtered.reshape(NEW, PLANES * CY * CZ)
    alive_flat = alive.reshape(PLANES)
    scaled = (mode_scales[:, None, None, None] * old_modes.astype(jnp.float32) * alive_flat[None, :, None, None]).astype(jnp.bfloat16)
    stacked = jnp.concatenate([filtered, scaled.reshape(KEEP, PLANES * CY * CZ)], axis=0)
    gram = jnp.dot(stacked.astype(jnp.float32), stacked.T.astype(jnp.float32), preferred_element_type=jnp.float32) / CELLS
    factor = jnp.linalg.cholesky(gram).T
    inverse = jax.scipy.linalg.solve_triangular(factor, jnp.eye(COLS, dtype=jnp.float32), lower=False)
    result = jnp.dot(inverse.T, stacked.astype(jnp.float32), precision=lax.Precision.HIGHEST)
    return (result.reshape(COLS, PLANES, CY, CZ).astype(jnp.bfloat16), factor)
```

```python
import functools

import jax
import jax.numpy as jnp
from jax import lax
from jax.experimental import pallas as pl
from jax.experimental.pallas import tpu as pltpu
from jax.sharding import PartitionSpec as P

PANEL = 64
VMEM_BYTES = 48 * 1024 * 1024


def stack_kernel(rows_y, snap_ref, modes_ref, scale_ref, left_ref, right_ref, count_ref, link_ref,
                 stacked_ref, gram_ref, snap_tmp, mode_tmp):
    new, planes, _, rows_z = snap_ref.shape
    keep = modes_ref.shape[0]
    alive1 = (count_ref[0] > 1).astype(jnp.float32)
    link0 = link_ref[0, 0].astype(jnp.float32)
    link1 = link_ref[0, 1].astype(jnp.float32)
    lane = lax.broadcasted_iota(jnp.int32, (new, rows_z), 1)

    for p in range(planes):
        alive = jnp.float32(1.0) if p == 0 else alive1
        scaled = modes_ref[:, p].astype(jnp.float32) * (scale_ref[...] * alive)[:, :, None]
        mode_tmp[...] = scaled.reshape(keep * rows_y, rows_z)
        for y in range(rows_y):
            part = mode_tmp[pl.ds(y, keep, stride=rows_y), :]
            at = (p * rows_y + y) * rows_z
            stacked_ref[new:, at:at + rows_z] = part.astype(jnp.bfloat16)

    x0 = snap_ref[:, 0].astype(jnp.float32)
    x1 = snap_ref[:, 1].astype(jnp.float32) * alive1
    right = right_ref[...].astype(jnp.float32) * link1
    left = left_ref[...].astype(jnp.float32) * link0
    along0 = 0.25 * left + 0.5 * x0 + 0.25 * (x1 + (1.0 - alive1) * right)
    along1 = alive1 * (0.25 * x0 + 0.5 * x1 + 0.25 * right)
    for p, along in ((0, along0), (1, along1)):
        snap_tmp[...] = along.reshape(new * rows_y, rows_z)
        lines = [snap_tmp[pl.ds(y, new, stride=rows_y), :] for y in range(rows_y)]
        for y in range(rows_y):
            value = 0.5 * lines[y]
            if y > 0:
                value = value + 0.25 * lines[y - 1]
            if y + 1 < rows_y:
                value = value + 0.25 * lines[y + 1]
            lower = jnp.where(lane == 0, 0.0, pltpu.roll(value, 1, 1))
            upper = jnp.where(lane == rows_z - 1, 0.0, pltpu.roll(value, rows_z - 1, 1))
            value = 0.25 * lower + 0.5 * value + 0.25 * upper
            at = (p * rows_y + y) * rows_z
            stacked_ref[:new, at:at + rows_z] = value.astype(jnp.bfloat16)

    gram_ref[...] = lax.dot_general(
        stacked_ref[...], stacked_ref[...], (((1,), (1,)), ((), ())),
        preferred_element_type=jnp.float32)


def inverse_of(x):
    guess = pl.reciprocal(x, approx=True)
    return guess * (2.0 - x * guess)


def lanes(x, j):
    return jnp.broadcast_to(x[:, j:j + 1], (8, 2 * PANEL))


def leaf(block):
    n = PANEL
    eye = (lax.broadcasted_iota(jnp.int32, (n, n), 0)
           == lax.broadcasted_iota(jnp.int32, (n, n), 1)).astype(jnp.float32)
    work = jnp.concatenate([block, eye], axis=1)
    tiles = [work[8 * t:8 * t + 8] for t in range(n // 8)]
    sub = lax.broadcasted_iota(jnp.int32, (8, 2 * n), 0)
    for j in range(0, n, 2):
        t0, s = divmod(j, 8)
        row0 = jnp.broadcast_to(tiles[t0][s:s + 1], (8, 2 * n))
        row1 = jnp.broadcast_to(tiles[t0][s + 1:s + 2], (8, 2 * n))
        a, b, c = lanes(row0, j), lanes(row0, j + 1), lanes(row1, j + 1)
        scale = inverse_of(a * c - b * b)
        first = (c * row0 - b * row1) * scale
        second = (a * row1 - b * row0) * scale
        for t in range(t0, n // 8):
            step = lanes(tiles[t], j) * first + lanes(tiles[t], j + 1) * second
            if t == t0:
                step = jnp.where(sub > s + 1, step, 0.0)
                step = jnp.where(sub == s + 1, b * inverse_of(a) * row0, step)
            tiles[t] = tiles[t] - step
    work = jnp.concatenate(tiles, axis=0)
    pick = (lax.broadcasted_iota(jnp.int32, (n, 2 * n), 0)
            == lax.broadcasted_iota(jnp.int32, (n, 2 * n), 1))
    diagonal = jnp.sum(jnp.where(pick, work, 0.0), axis=1, keepdims=True)
    work = work * lax.rsqrt(diagonal)
    row = lax.broadcasted_iota(jnp.int32, (n, n), 0)
    col = lax.broadcasted_iota(jnp.int32, (n, n), 1)
    return jnp.where(col >= row, work[:, :n], 0.0), work[:, n:]


def factor_kernel(inv_cells, rows_y, gram_ref, stacked_hbm, out_ref, factor_ref,
                  stacked, packed, inverse, tmp, sem):
    load = pltpu.make_async_copy(stacked_hbm, stacked, sem)
    load.start()
    order = gram_ref.shape[0]
    rows_z = out_ref.shape[3]
    exact = functools.partial(lax.dot_general, precision=lax.Precision.HIGHEST,
                              preferred_element_type=jnp.float32)
    packed[...] = gram_ref[...] * inv_cells
    col = lax.broadcasted_iota(jnp.int32, (1, order), 1)
    for at in range(0, order, PANEL):
        end = at + PANEL
        upper, low_inv = leaf(packed[at:end, at:end])
        inside = (col >= at) & (col < end)
        top = exact(low_inv, packed[at:end, :], (((1,), (0,)), ((), ())))
        spread = jnp.concatenate(
            [low_inv if q == at else jnp.zeros_like(low_inv) for q in range(0, order, PANEL)], axis=1)
        top = jnp.where(inside, spread, top)
        inverse[at:end, :] = jnp.where(col < end, top, 0.0)
        placed = jnp.concatenate(
            [upper if q == at else jnp.zeros_like(upper) for q in range(0, order, PANEL)], axis=1)
        factor_ref[at:end, :] = jnp.where(col >= end, top, placed)
        if end < order:
            update = exact(top[:, end:], top, (((0,), (0,)), ((), ())))
            packed[end:, :] = jnp.where(inside, 0.0, packed[end:, :]) - update

    full = inverse[...]
    high = full.astype(jnp.bfloat16)
    low = (full - high.astype(jnp.float32)).astype(jnp.bfloat16)
    load.wait()
    for p in range(out_ref.shape[1]):
        for y in range(0, rows_y, 2):
            at = (p * rows_y + y) * rows_z
            part = stacked[:, at:at + 2 * rows_z]
            value = (jnp.dot(high, part, preferred_element_type=jnp.float32)
                     + jnp.dot(low, part, preferred_element_type=jnp.float32))
            tmp[pl.ds(y, order, stride=rows_y), :] = value[:, :rows_z]
            tmp[pl.ds(y + 1, order, stride=rows_y), :] = value[:, rows_z:]
        out_ref[:, p] = tmp[...].reshape(order, rows_y, rows_z).astype(jnp.bfloat16)


def shards(snapshots, old_modes, mode_scales, plane_counts, links):
    new, planes, rows_y, rows_z = snapshots.shape
    keep = old_modes.shape[0]
    order = new + keep
    cells = planes * rows_y * rows_z
    peers = lax.axis_size("blk")
    up = [(i, (i + 1) % peers) for i in range(peers)]
    down = [(j, i) for i, j in up]
    first = snapshots[:, 0]
    last = jnp.where(plane_counts[0] > 1, snapshots[:, 1], snapshots[:, 0])
    left = lax.ppermute(last, "blk", up)
    right = lax.ppermute(first, "blk", down)
    vmem = pl.BlockSpec(memory_space=pltpu.VMEM)
    smem = pl.BlockSpec(memory_space=pltpu.SMEM)
    stacked, gram = pl.pallas_call(
        functools.partial(stack_kernel, rows_y),
        out_shape=(jax.ShapeDtypeStruct((order, cells), jnp.bfloat16),
                   jax.ShapeDtypeStruct((order, order), jnp.float32)),
        in_specs=[vmem] * 5 + [smem] * 2,
        out_specs=(vmem, vmem),
        scratch_shapes=[pltpu.VMEM((new * rows_y, rows_z), jnp.float32),
                        pltpu.VMEM((keep * rows_y, rows_z), jnp.float32)],
        compiler_params=pltpu.CompilerParams(vmem_limit_bytes=VMEM_BYTES),
        name="stack",
    )(snapshots, old_modes, mode_scales[:, None], left, right, plane_counts, links)
    gram = lax.psum(gram, "blk")
    new_modes, factor = pl.pallas_call(
        functools.partial(factor_kernel, 1.0 / (peers * cells), rows_y),
        out_shape=(jax.ShapeDtypeStruct((order, planes, rows_y, rows_z), jnp.bfloat16),
                   jax.ShapeDtypeStruct((order, order), jnp.float32)),
        in_specs=[vmem, pl.BlockSpec(memory_space=pl.ANY)],
        out_specs=(vmem, vmem),
        scratch_shapes=[pltpu.VMEM((order, cells), jnp.bfloat16),
                        pltpu.VMEM((order, order), jnp.float32),
                        pltpu.VMEM((order, order), jnp.float32),
                        pltpu.VMEM((order * rows_y, rows_z), jnp.float32),
                        pltpu.SemaphoreType.DMA],
        compiler_params=pltpu.CompilerParams(vmem_limit_bytes=VMEM_BYTES),
        name="factor",
    )(gram, stacked)
    return (new_modes, factor)


def solution(mesh):
    return jax.shard_map(
        shards,
        mesh=mesh,
        in_specs=(
            P(None, ("groups", "blk"), None, None),
            P(None, ("groups", "blk"), None, None),
            P("groups"),
            P(("groups", "blk")),
            P(("groups", "blk"), None),
        ),
        out_specs=(P(None, ("groups", "blk"), None, None), P("groups", None)),
        check_vma=False,
    )
```

```python
import functools

import jax
import jax.numpy as jnp
from jax import lax
from jax.experimental import pallas as pl
from jax.experimental.pallas import tpu as pltpu
from jax.sharding import PartitionSpec as P

PANEL = 64
VMEM_BYTES = 48 * 1024 * 1024


def levels_of(peers, rows):
    found, stride = [], 1
    while stride < peers:
        left = peers // stride
        radix = next((r for r in (4, 2) if left % r == 0), left)
        kept = rows // radix if rows % (8 * radix) == 0 else rows
        found.append((stride, radix, rows, kept))
        stride, rows = stride * radix, kept
    return found


def stack_kernel(levels, peers, scale_ref, count_ref, link_ref, snap_hbm, modes_hbm,
                 stacked_ref, gram_ref, snap, modes, last, left_in, right_in, snap_tmp, mode_tmp,
                 total, load_sem, halo_sem, sum_sem, *buffers):
    new, planes, rows_y, rows_z = snap.shape
    keep = modes.shape[0]
    half = stacked_ref.shape[0] // 2
    parts = buffers[:len(levels) + 1]
    inbox = buffers[len(levels) + 1:]
    me = lax.axis_index("blk")

    load_snap = pltpu.make_async_copy(snap_hbm, snap, load_sem.at[0])
    load_modes = pltpu.make_async_copy(modes_hbm, modes, load_sem.at[1])
    load_snap.start()
    load_modes.start()

    above, below = (me + 1) % peers, (me + peers - 1) % peers
    partners = [above, below]
    for stride, radix, _, _ in levels:
        digit = (me // stride) % radix
        partners += [me + ((digit + k) % radix - digit) * stride for k in range(1, radix)]
    barrier = pltpu.get_barrier_semaphore()
    for partner in partners:
        pl.semaphore_signal(barrier, inc=1, device_id={"blk": partner},
                            device_id_type=pl.DeviceIdType.MESH)

    alive1 = (count_ref[0] > 1).astype(jnp.float32)
    link0 = link_ref[0, 0].astype(jnp.float32)
    link1 = link_ref[0, 1].astype(jnp.float32)
    lane = lax.broadcasted_iota(jnp.int32, (new, rows_z), 1)

    load_snap.wait()
    last[...] = (snap[:, 1].astype(jnp.float32) * alive1
                 + snap[:, 0].astype(jnp.float32) * (1.0 - alive1)).astype(jnp.bfloat16)
    pl.semaphore_wait(barrier, len(partners))
    send_up = pltpu.make_async_remote_copy(
        last, left_in, halo_sem.at[0, 0], halo_sem.at[0, 1],
        device_id={"blk": above}, device_id_type=pl.DeviceIdType.MESH)
    send_down = pltpu.make_async_remote_copy(
        snap.at[:, 0], right_in, halo_sem.at[1, 0], halo_sem.at[1, 1],
        device_id={"blk": below}, device_id_type=pl.DeviceIdType.MESH)
    send_up.start()
    send_down.start()

    eye = (lax.broadcasted_iota(jnp.int32, (keep, keep), 0)
           == lax.broadcasted_iota(jnp.int32, (keep, keep), 1))
    scale = jnp.sum(jnp.where(eye, scale_ref[...], 0.0), axis=1, keepdims=True)
    load_modes.wait()
    for p in range(planes):
        mode_tmp[...] = modes[:, p].astype(jnp.float32).reshape(keep * rows_y, rows_z)
        weight = jnp.broadcast_to(scale if p == 0 else scale * alive1, (keep, rows_z))
        for y in range(rows_y):
            part = mode_tmp[pl.ds(y, keep, stride=rows_y), :] * weight
            at = (p * rows_y + y) * rows_z
            stacked_ref[new:, at:at + rows_z] = part.astype(jnp.bfloat16)
    tail = stacked_ref[half:, :]
    parts[0][:, 2 * half:] = lax.dot_general(
        tail, tail, (((1,), (1,)), ((), ())), preferred_element_type=jnp.float32)

    x0 = snap[:, 0].astype(jnp.float32)
    x1 = snap[:, 1].astype(jnp.float32) * alive1
    send_up.wait_recv()
    send_down.wait_recv()
    right = right_in[...].astype(jnp.float32) * link1
    left = left_in[...].astype(jnp.float32) * link0
    along0 = 0.25 * left + 0.5 * x0 + 0.25 * (x1 + (1.0 - alive1) * right)
    along1 = alive1 * (0.25 * x0 + 0.5 * x1 + 0.25 * right)
    for p, along in ((0, along0), (1, along1)):
        snap_tmp[...] = along.reshape(new * rows_y, rows_z)
        lines = [snap_tmp[pl.ds(y, new, stride=rows_y), :] for y in range(rows_y)]
        for y in range(rows_y):
            value = 0.5 * lines[y]
            if y > 0:
                value = value + 0.25 * lines[y - 1]
            if y + 1 < rows_y:
                value = value + 0.25 * lines[y + 1]
            lower = jnp.where(lane == 0, 0.0, pltpu.roll(value, 1, 1))
            upper = jnp.where(lane == rows_z - 1, 0.0, pltpu.roll(value, rows_z - 1, 1))
            value = 0.25 * lower + 0.5 * value + 0.25 * upper
            at = (p * rows_y + y) * rows_z
            stacked_ref[:new, at:at + rows_z] = value.astype(jnp.bfloat16)
    parts[0][:, :2 * half] = lax.dot_general(
        stacked_ref[:half, :], stacked_ref[...], (((1,), (1,)), ((), ())),
        preferred_element_type=jnp.float32)

    sends, base, bases = [send_up, send_down], 0, [0]
    for level, (stride, radix, rows, kept) in enumerate(levels):
        digit = (me // stride) % radix
        split = kept < rows
        copies = []
        for k in range(1, radix):
            other = (digit + k) % radix
            start = pl.multiple_of(other * kept, 8) if split else 0
            copy = pltpu.make_async_remote_copy(
                parts[level].at[pl.ds(start, kept), :], inbox[level].at[k - 1],
                sum_sem.at[level, 0, k - 1, 0], sum_sem.at[level, 0, k - 1, 1],
                device_id={"blk": me + (other - digit) * stride},
                device_id_type=pl.DeviceIdType.MESH)
            copy.start()
            copies.append(copy)
        own = pl.multiple_of(digit * kept, 8) if split else 0
        value = parts[level][pl.ds(own, kept), :]
        for k, copy in enumerate(copies):
            copy.wait_recv()
            value = value + inbox[level][k]
        parts[level + 1][...] = value
        base = base + own
        bases.append(base)
        sends += copies

    kept = levels[-1][3]
    total[pl.ds(pl.multiple_of(base, 8), kept), :] = parts[-1][...]
    for level in reversed(range(len(levels))):
        stride, radix, rows, kept = levels[level]
        if kept == rows:
            continue
        digit = (me // stride) % radix
        piece = total.at[pl.ds(pl.multiple_of(bases[level + 1], 8), kept), :]
        copies = []
        for k in range(1, radix):
            other = (digit + k) % radix
            copy = pltpu.make_async_remote_copy(
                piece, piece, sum_sem.at[level, 1, k - 1, 0], sum_sem.at[level, 1, k - 1, 1],
                device_id={"blk": me + (other - digit) * stride},
                device_id_type=pl.DeviceIdType.MESH)
            copy.start()
            copies.append(copy)
        for copy in copies:
            copy.wait_recv()
        sends += copies
    gram_ref[...] = total[...]
    for copy in sends:
        copy.wait_send()


def inverse_of(x):
    guess = pl.reciprocal(x, approx=True)
    return guess * (2.0 - x * guess)


def lanes(x, j):
    return jnp.broadcast_to(x[:, j:j + 1], (8, 2 * PANEL))


def leaf(block):
    n = PANEL
    eye = (lax.broadcasted_iota(jnp.int32, (n, n), 0)
           == lax.broadcasted_iota(jnp.int32, (n, n), 1)).astype(jnp.float32)
    work = jnp.concatenate([block, eye], axis=1)
    tiles = [work[8 * t:8 * t + 8] for t in range(n // 8)]
    sub = lax.broadcasted_iota(jnp.int32, (8, 2 * n), 0)
    for j in range(0, n, 2):
        t0, s = divmod(j, 8)
        row0 = jnp.broadcast_to(tiles[t0][s:s + 1], (8, 2 * n))
        row1 = jnp.broadcast_to(tiles[t0][s + 1:s + 2], (8, 2 * n))
        a, b, c = lanes(row0, j), lanes(row0, j + 1), lanes(row1, j + 1)
        scale = inverse_of(a * c - b * b)
        first = (c * row0 - b * row1) * scale
        second = (a * row1 - b * row0) * scale
        for t in range(t0, n // 8):
            step = lanes(tiles[t], j) * first + lanes(tiles[t], j + 1) * second
            if t == t0:
                step = jnp.where(sub > s + 1, step, 0.0)
                step = jnp.where(sub == s + 1, b * inverse_of(a) * row0, step)
            tiles[t] = tiles[t] - step
    work = jnp.concatenate(tiles, axis=0)
    pick = (lax.broadcasted_iota(jnp.int32, (n, 2 * n), 0)
            == lax.broadcasted_iota(jnp.int32, (n, 2 * n), 1))
    diagonal = jnp.sum(jnp.where(pick, work, 0.0), axis=1, keepdims=True)
    work = work * lax.rsqrt(diagonal)
    row = lax.broadcasted_iota(jnp.int32, (n, n), 0)
    col = lax.broadcasted_iota(jnp.int32, (n, n), 1)
    return jnp.where(col >= row, work[:, :n], 0.0), work[:, n:]


def factor_kernel(inv_cells, rows_y, gram_ref, stacked_hbm, out_ref, factor_ref,
                  stacked, packed, inverse, tmp, sem):
    load = pltpu.make_async_copy(stacked_hbm, stacked, sem)
    load.start()
    order = out_ref.shape[0]
    rows_z = out_ref.shape[3]
    exact = functools.partial(lax.dot_general, precision=lax.Precision.HIGHEST,
                              preferred_element_type=jnp.float32)
    half = order // 2
    packed[:half, :] = gram_ref[:, :order] * inv_cells
    packed[half:, :half] = jnp.zeros((half, half), jnp.float32)
    packed[half:, half:] = gram_ref[:, order:] * inv_cells
    col = lax.broadcasted_iota(jnp.int32, (1, order), 1)
    for at in range(0, order, PANEL):
        end = at + PANEL
        upper, low_inv = leaf(packed[at:end, at:end])
        inside = (col >= at) & (col < end)
        top = exact(low_inv, packed[at:end, :], (((1,), (0,)), ((), ())))
        spread = jnp.concatenate(
            [low_inv if q == at else jnp.zeros_like(low_inv) for q in range(0, order, PANEL)], axis=1)
        top = jnp.where(inside, spread, top)
        inverse[at:end, :] = jnp.where(col < end, top, 0.0)
        placed = jnp.concatenate(
            [upper if q == at else jnp.zeros_like(upper) for q in range(0, order, PANEL)], axis=1)
        factor_ref[at:end, :] = jnp.where(col >= end, top, placed)
        if end < order:
            update = exact(top[:, end:], top, (((0,), (0,)), ((), ())))
            packed[end:, :] = jnp.where(inside, 0.0, packed[end:, :]) - update

    full = inverse[...]
    high = full.astype(jnp.bfloat16)
    low = (full - high.astype(jnp.float32)).astype(jnp.bfloat16)
    load.wait()
    for p in range(out_ref.shape[1]):
        for y in range(0, rows_y, 2):
            at = (p * rows_y + y) * rows_z
            part = stacked[:, at:at + 2 * rows_z]
            value = (jnp.dot(high, part, preferred_element_type=jnp.float32)
                     + jnp.dot(low, part, preferred_element_type=jnp.float32))
            tmp[pl.ds(y, order, stride=rows_y), :] = value[:, :rows_z]
            tmp[pl.ds(y + 1, order, stride=rows_y), :] = value[:, rows_z:]
        out_ref[:, p] = tmp[...].reshape(order, rows_y, rows_z).astype(jnp.bfloat16)


def shards(snapshots, old_modes, mode_scales, plane_counts, links):
    new, planes, rows_y, rows_z = snapshots.shape
    keep = old_modes.shape[0]
    order = new + keep
    cells = planes * rows_y * rows_z
    peers = lax.axis_size("blk")
    levels = levels_of(peers, order // 2)
    radix = max(level[1] for level in levels)
    packed = lambda rows: pltpu.VMEM((rows, 3 * order // 2), jnp.float32)
    vmem = pl.BlockSpec(memory_space=pltpu.VMEM)
    smem = pl.BlockSpec(memory_space=pltpu.SMEM)
    hbm = pl.BlockSpec(memory_space=pl.ANY)
    plane = pltpu.VMEM((new, rows_y, rows_z), jnp.bfloat16)
    stacked, gram = pl.pallas_call(
        functools.partial(stack_kernel, levels, peers),
        out_shape=(jax.ShapeDtypeStruct((order, cells), jnp.bfloat16),
                   jax.ShapeDtypeStruct((order // 2, 3 * order // 2), jnp.float32)),
        in_specs=[vmem, smem, smem, hbm, hbm],
        out_specs=(vmem, vmem),
        scratch_shapes=[pltpu.VMEM(snapshots.shape, jnp.bfloat16),
                        pltpu.VMEM(old_modes.shape, jnp.bfloat16),
                        plane, plane, plane,
                        pltpu.VMEM((new * rows_y, rows_z), jnp.float32),
                        pltpu.VMEM((keep * rows_y, rows_z), jnp.float32),
                        packed(order // 2),
                        pltpu.SemaphoreType.DMA((2,)),
                        pltpu.SemaphoreType.DMA((2, 2)),
                        pltpu.SemaphoreType.DMA((len(levels), 2, radix - 1, 2)),
                        packed(order // 2), *[packed(level[3]) for level in levels],
                        *[pltpu.VMEM((level[1] - 1, level[3], 3 * order // 2), jnp.float32)
                          for level in levels]],
        compiler_params=pltpu.CompilerParams(
            vmem_limit_bytes=VMEM_BYTES, collective_id=0, has_side_effects=True),
        name="stack",
    )(mode_scales.reshape(1, keep), plane_counts, links, snapshots, old_modes)
    new_modes, factor = pl.pallas_call(
        functools.partial(factor_kernel, 1.0 / (peers * cells), rows_y),
        out_shape=(jax.ShapeDtypeStruct((order, planes, rows_y, rows_z), jnp.bfloat16),
                   jax.ShapeDtypeStruct((order, order), jnp.float32)),
        in_specs=[vmem, hbm],
        out_specs=(vmem, vmem),
        scratch_shapes=[pltpu.VMEM((order, cells), jnp.bfloat16),
                        pltpu.VMEM((order, order), jnp.float32),
                        pltpu.VMEM((order, order), jnp.float32),
                        pltpu.VMEM((order * rows_y, rows_z), jnp.float32),
                        pltpu.SemaphoreType.DMA],
        compiler_params=pltpu.CompilerParams(vmem_limit_bytes=VMEM_BYTES),
        name="factor",
    )(gram, stacked)
    return (new_modes, factor)


def solution(mesh):
    return jax.shard_map(
        shards,
        mesh=mesh,
        in_specs=(
            P(None, ("groups", "blk"), None, None),
            P(None, ("groups", "blk"), None, None),
            P("groups"),
            P(("groups", "blk")),
            P(("groups", "blk"), None),
        ),
        out_specs=(P(None, ("groups", "blk"), None, None), P("groups", None)),
        check_vma=False,
    )
```

```python
import functools

import jax
import jax.numpy as jnp
from jax import lax
from jax.experimental import pallas as pl
from jax.experimental.pallas import tpu as pltpu
from jax.sharding import PartitionSpec as P

PANEL = 64
VMEM_BYTES = 62 * 1024 * 1024


def levels_of(peers, rows):
    found, stride = [], 1
    while stride < peers:
        left = peers // stride
        radix = next((r for r in (4, 2) if left % r == 0), left)
        kept = rows // radix if rows % (8 * radix) == 0 else rows
        found.append((stride, radix, rows, kept))
        stride, rows = stride * radix, kept
    return found


class Exchange:
    def __init__(self, levels, me, parts, inbox, total, sems):
        self.levels, self.me = levels, me
        self.parts, self.inbox, self.total, self.sems = parts, inbox, total, sems
        self.stages = [(level, 0) for level in range(len(levels))]
        self.stages += [(level, 1) for level in reversed(range(len(levels)))
                        if levels[level][3] < levels[level][2]]
        self.base = [0]
        for stride, radix, rows, kept in levels:
            own = ((me // stride) % radix) * kept if kept < rows else 0
            self.base.append(self.base[-1] + own)
        self.at, self.copies, self.sends = 0, [], []

    def start(self):
        level, phase = self.stages[self.at]
        stride, radix, rows, kept = self.levels[level]
        digit = (self.me // stride) % radix
        if phase == 1 and not self.stages[self.at - 1][1]:
            first = pl.multiple_of(self.base[-1], 8)
            self.total[pl.ds(first, self.levels[-1][3]), :] = self.parts[-1][...]
        self.copies = []
        for k in range(1, radix):
            other = (digit + k) % radix
            if phase == 0:
                first = pl.multiple_of(other * kept, 8) if kept < rows else 0
                source = self.parts[level].at[pl.ds(first, kept), :]
                target = self.inbox[level].at[k - 1]
            else:
                first = pl.multiple_of(self.base[level + 1], 8)
                source = target = self.total.at[pl.ds(first, kept), :]
            copy = pltpu.make_async_remote_copy(
                source, target, self.sems.at[level, phase, k - 1, 0],
                self.sems.at[level, phase, k - 1, 1],
                device_id={"blk": self.me + (other - digit) * stride},
                device_id_type=pl.DeviceIdType.MESH)
            copy.start()
            self.copies.append(copy)
        self.sends += self.copies

    def finish(self):
        level, phase = self.stages[self.at]
        stride, radix, rows, kept = self.levels[level]
        if phase == 0:
            own = pl.multiple_of(((self.me // stride) % radix) * kept, 8) if kept < rows else 0
            value = self.parts[level][pl.ds(own, kept), :]
        for k, copy in enumerate(self.copies):
            copy.wait_recv()
            if phase == 0:
                value = value + self.inbox[level][k]
        if phase == 0:
            self.parts[level + 1][...] = value
        self.at += 1

    def advance(self):
        if self.at < len(self.stages):
            self.finish()
            if self.at < len(self.stages):
                self.start()


def stack_kernel(levels, peers, scale_hbm, count_hbm, link_hbm, snap_hbm, modes_hbm,
                 stacked_hbm, gram_new, gram_old, scale_ref, count_ref, link_ref, snap, modes, last, left_in, right_in, snap_tmp, mode_tmp,
                 stacked_ref, total_new, total_old, load_sem, halo_sem, sum_sem, *buffers):
    new, planes, rows_y, rows_z = snap.shape
    keep = modes.shape[0]
    me = lax.axis_index("blk")
    count = 2 * len(levels) + 1
    old_sum, new_sum = [
        Exchange(levels, me, buffers[i * count:i * count + len(levels) + 1],
                 buffers[i * count + len(levels) + 1:(i + 1) * count], total, sum_sem.at[i])
        for i, total in enumerate((total_old, total_new))]

    load_snap = pltpu.make_async_copy(snap_hbm, snap, load_sem.at[0])
    load_modes = pltpu.make_async_copy(modes_hbm, modes, load_sem.at[1])
    small = [pltpu.make_async_copy(source, target, load_sem.at[2 + i]) for i, (source, target) in
             enumerate(((count_hbm, count_ref), (link_hbm, link_ref), (scale_hbm, scale_ref)))]
    load_snap.start()
    for copy in small:
        copy.start()
    load_modes.start()

    above, below = (me + 1) % peers, (me + peers - 1) % peers
    partners = [above, below]
    for stride, radix, _, _ in levels:
        digit = (me // stride) % radix
        partners += [me + ((digit + k) % radix - digit) * stride for k in range(1, radix)]
    barrier = pltpu.get_barrier_semaphore()
    for partner in partners:
        pl.semaphore_signal(barrier, inc=1, device_id={"blk": partner},
                            device_id_type=pl.DeviceIdType.MESH)

    for copy in small:
        copy.wait()
    alive1 = (count_ref[0] > 1).astype(jnp.float32)
    link0 = link_ref[0, 0].astype(jnp.float32)
    link1 = link_ref[0, 1].astype(jnp.float32)
    lane = lax.broadcasted_iota(jnp.int32, (new, rows_z), 1)

    load_snap.wait()
    last[...] = (snap[:, 1].astype(jnp.float32) * alive1
                 + snap[:, 0].astype(jnp.float32) * (1.0 - alive1)).astype(jnp.bfloat16)
    pl.semaphore_wait(barrier, len(partners))
    send_up = pltpu.make_async_remote_copy(
        last, left_in, halo_sem.at[0, 0], halo_sem.at[0, 1],
        device_id={"blk": above}, device_id_type=pl.DeviceIdType.MESH)
    send_down = pltpu.make_async_remote_copy(
        snap.at[:, 0], right_in, halo_sem.at[1, 0], halo_sem.at[1, 1],
        device_id={"blk": below}, device_id_type=pl.DeviceIdType.MESH)
    send_up.start()
    send_down.start()

    eye = (lax.broadcasted_iota(jnp.int32, (keep, keep), 0)
           == lax.broadcasted_iota(jnp.int32, (keep, keep), 1))
    scale = jnp.sum(jnp.where(eye, scale_ref[...], 0.0), axis=1, keepdims=True)
    load_modes.wait()
    for p in range(planes):
        mode_tmp[...] = modes[:, p].astype(jnp.float32).reshape(keep * rows_y, rows_z)
        weight = jnp.broadcast_to(scale if p == 0 else scale * alive1, (keep, rows_z))
        for y in range(rows_y):
            part = mode_tmp[pl.ds(y, keep, stride=rows_y), :] * weight
            at = (p * rows_y + y) * rows_z
            stacked_ref[new:, at:at + rows_z] = part.astype(jnp.bfloat16)
    store_old = pltpu.make_async_copy(
        stacked_ref.at[pl.ds(new, keep), :], stacked_hbm.at[pl.ds(new, keep), :], load_sem.at[5])
    store_old.start()
    tail = stacked_ref[new:, :]
    gram = lax.dot_general(
        tail, tail, (((1,), (1,)), ((), ())), preferred_element_type=jnp.float32)
    at = 0
    for row in range(0, keep, new):
        old_sum.parts[0][:, at:at + keep - row] = gram[row:row + new, row:]
        at += keep - row
    old_sum.start()
    old_sum.advance()

    x0 = snap[:, 0].astype(jnp.float32)
    x1 = snap[:, 1].astype(jnp.float32) * alive1
    send_up.wait_recv()
    send_down.wait_recv()
    right = right_in[...].astype(jnp.float32) * link1
    left = left_in[...].astype(jnp.float32) * link0
    along0 = 0.25 * left + 0.5 * x0 + 0.25 * (x1 + (1.0 - alive1) * right)
    along1 = alive1 * (0.25 * x0 + 0.5 * x1 + 0.25 * right)
    for p, along in ((0, along0), (1, along1)):
        snap_tmp[...] = along.reshape(new * rows_y, rows_z)
        lines = [snap_tmp[pl.ds(y, new, stride=rows_y), :] for y in range(rows_y)]
        for y in range(rows_y):
            value = 0.5 * lines[y]
            if y > 0:
                value = value + 0.25 * lines[y - 1]
            if y + 1 < rows_y:
                value = value + 0.25 * lines[y + 1]
            lower = jnp.where(lane == 0, 0.0, pltpu.roll(value, 1, 1))
            upper = jnp.where(lane == rows_z - 1, 0.0, pltpu.roll(value, rows_z - 1, 1))
            value = 0.25 * lower + 0.5 * value + 0.25 * upper
            at = (p * rows_y + y) * rows_z
            stacked_ref[:new, at:at + rows_z] = value.astype(jnp.bfloat16)
    store_new = pltpu.make_async_copy(
        stacked_ref.at[pl.ds(0, new), :], stacked_hbm.at[pl.ds(0, new), :], load_sem.at[6])
    store_new.start()
    new_sum.parts[0][...] = lax.dot_general(
        stacked_ref[:new, :], stacked_ref[...], (((1,), (1,)), ((), ())),
        preferred_element_type=jnp.float32)
    new_sum.start()
    for _ in new_sum.stages:
        old_sum.advance()
        new_sum.advance()
    gram_new[...] = total_new[...]
    gram_old[...] = total_old[...]
    for copy in (send_up, send_down, *old_sum.sends, *new_sum.sends):
        copy.wait_send()
    store_old.wait()
    store_new.wait()


def inverse_of(x):
    guess = pl.reciprocal(x, approx=True)
    return guess * (2.0 - x * guess)


def lanes(x, j):
    return jnp.broadcast_to(x[:, j:j + 1], (8, 2 * PANEL))


def leaf(block):
    n = PANEL
    eye = (lax.broadcasted_iota(jnp.int32, (n, n), 0)
           == lax.broadcasted_iota(jnp.int32, (n, n), 1)).astype(jnp.float32)
    work = jnp.concatenate([block, eye], axis=1)
    tiles = [work[8 * t:8 * t + 8] for t in range(n // 8)]
    sub = lax.broadcasted_iota(jnp.int32, (8, 2 * n), 0)
    for t0 in range(n // 8):
        at = 8 * t0
        rows = [jnp.broadcast_to(tiles[t0][k:k + 1], (8, 2 * n)) for k in range(8)]
        pivots = [[lanes(rows[k], at + q) if q >= k else None for q in range(8)] for k in range(8)]
        others = range(t0 + 1, n // 8)
        sides = {t: [lanes(tiles[t], at + q) for q in range(8)] for t in others}
        for k in range(0, 8, 2):
            a, b, c = pivots[k][k], pivots[k][k + 1], pivots[k + 1][k + 1]
            scale = inverse_of(a * c - b * b)
            first = {q: (c * pivots[k][q] - b * pivots[k + 1][q]) * scale for q in range(k + 2, 8)}
            second = {q: (a * pivots[k + 1][q] - b * pivots[k][q]) * scale for q in range(k + 2, 8)}
            row_first = (c * rows[k] - b * rows[k + 1]) * scale
            row_second = (a * rows[k + 1] - b * rows[k]) * scale
            for r in range(k + 2, 8):
                x, y = pivots[k][r], pivots[k + 1][r]
                for q in range(r, 8):
                    pivots[r][q] = pivots[r][q] - (x * first[q] + y * second[q])
                rows[r] = rows[r] - (x * row_first + y * row_second)
            for t in others:
                x, y = sides[t][k], sides[t][k + 1]
                for q in range(k + 2, 8):
                    sides[t][q] = sides[t][q] - (x * first[q] + y * second[q])
                tiles[t] = tiles[t] - (x * row_first + y * row_second)
            rows[k + 1] = rows[k + 1] - b * inverse_of(a) * rows[k]
        done = rows[0]
        for k in range(1, 8):
            done = jnp.where(sub == k, rows[k], done)
        tiles[t0] = done
    work = jnp.concatenate(tiles, axis=0)
    pick = (lax.broadcasted_iota(jnp.int32, (n, 2 * n), 0)
            == lax.broadcasted_iota(jnp.int32, (n, 2 * n), 1))
    diagonal = jnp.sum(jnp.where(pick, work, 0.0), axis=1, keepdims=True)
    work = work * lax.rsqrt(diagonal)
    row = lax.broadcasted_iota(jnp.int32, (n, n), 0)
    col = lax.broadcasted_iota(jnp.int32, (n, n), 1)
    return jnp.where(col >= row, work[:, :n], 0.0), work[:, n:]


def factor_kernel(inv_cells, gram_new, gram_old, stacked_hbm, out_hbm, factor_ref,
                  stacked, packed, inverse, tmp, stage, sem):
    load = pltpu.make_async_copy(stacked_hbm, stacked, sem.at[0])
    load.start()
    order, planes, rows_y, rows_z = out_hbm.shape
    new = gram_new.shape[0]
    exact = functools.partial(lax.dot_general, precision=lax.Precision.HIGHEST,
                              preferred_element_type=jnp.float32)
    packed[:new, :] = gram_new[...] * inv_cells
    packed[new:, :] = jnp.zeros((order - new, order), jnp.float32)
    at = 0
    for row in range(new, order, new):
        packed[row:row + new, row:] = gram_old[:, at:at + order - row] * inv_cells
        at += order - row
    col = lax.broadcasted_iota(jnp.int32, (1, order), 1)
    for at in range(0, order, PANEL):
        end = at + PANEL
        upper, low_inv = leaf(packed[at:end, at:end])
        inside = (col >= at) & (col < end)
        top = exact(low_inv, packed[at:end, :], (((1,), (0,)), ((), ())))
        spread = jnp.concatenate(
            [low_inv if q == at else jnp.zeros_like(low_inv) for q in range(0, order, PANEL)], axis=1)
        top = jnp.where(inside, spread, top)
        inverse[at:end, :] = jnp.where(col < end, top, 0.0)
        placed = jnp.concatenate(
            [upper if q == at else jnp.zeros_like(upper) for q in range(0, order, PANEL)], axis=1)
        factor_ref[at:end, :] = jnp.where(col >= end, top, placed)
        if end < order:
            update = exact(top[:, end:], top, (((0,), (0,)), ((), ())))
            packed[end:, :] = jnp.where(inside, 0.0, packed[end:, :]) - update

    full = inverse[...]
    high = full.astype(jnp.bfloat16)
    low = (full - high.astype(jnp.float32)).astype(jnp.bfloat16)
    load.wait()
    stores = []
    for p in range(planes):
        for y in range(0, rows_y, 2):
            at = (p * rows_y + y) * rows_z
            part = stacked[:, at:at + 2 * rows_z]
            value = (jnp.dot(high, part, preferred_element_type=jnp.float32)
                     + jnp.dot(low, part, preferred_element_type=jnp.float32))
            tmp[pl.ds(y, order, stride=rows_y), :] = value[:, :rows_z]
            tmp[pl.ds(y + 1, order, stride=rows_y), :] = value[:, rows_z:]
        stage[p] = tmp[...].reshape(order, rows_y, rows_z).astype(jnp.bfloat16)
        store = pltpu.make_async_copy(stage.at[p], out_hbm.at[:, p], sem.at[1 + p])
        store.start()
        stores.append(store)
    for store in stores:
        store.wait()


def shards(snapshots, old_modes, mode_scales, plane_counts, links):
    new, planes, rows_y, rows_z = snapshots.shape
    keep = old_modes.shape[0]
    order = new + keep
    cells = planes * rows_y * rows_z
    peers = lax.axis_size("blk")
    levels = levels_of(peers, new)
    radix = max(level[1] for level in levels)
    widths = (sum(range(new, keep + 1, new)), order)
    sums = [pltpu.VMEM(shape, jnp.float32) for width in widths for shape in (
        [(new, width)] + [(level[3], width) for level in levels]
        + [(level[1] - 1, level[3], width) for level in levels])]
    vmem = pl.BlockSpec(memory_space=pltpu.VMEM)
    smem = pl.BlockSpec(memory_space=pltpu.SMEM)
    hbm = pl.BlockSpec(memory_space=pltpu.HBM)
    plane = pltpu.VMEM((new, rows_y, rows_z), jnp.bfloat16)
    stacked, gram_new, gram_old = pl.pallas_call(
        functools.partial(stack_kernel, levels, peers),
        out_shape=(jax.ShapeDtypeStruct((order, cells), jnp.bfloat16),
                   jax.ShapeDtypeStruct((new, widths[1]), jnp.float32),
                   jax.ShapeDtypeStruct((new, widths[0]), jnp.float32)),
        in_specs=[hbm] * 5,
        out_specs=(hbm, vmem, vmem),
        scratch_shapes=[pltpu.VMEM((1, keep), jnp.float32),
                        pltpu.SMEM(plane_counts.shape, jnp.int32),
                        pltpu.SMEM(links.shape, jnp.int32),
                        pltpu.VMEM(snapshots.shape, jnp.bfloat16),
                        pltpu.VMEM(old_modes.shape, jnp.bfloat16),
                        plane, plane, plane,
                        pltpu.VMEM((new * rows_y, rows_z), jnp.float32),
                        pltpu.VMEM((keep * rows_y, rows_z), jnp.float32),
                        pltpu.VMEM((order, cells), jnp.bfloat16),
                        pltpu.VMEM((new, widths[1]), jnp.float32),
                        pltpu.VMEM((new, widths[0]), jnp.float32),
                        pltpu.SemaphoreType.DMA((7,)),
                        pltpu.SemaphoreType.DMA((2, 2)),
                        pltpu.SemaphoreType.DMA((2, len(levels), 2, radix - 1, 2)), *sums],
        compiler_params=pltpu.CompilerParams(
            vmem_limit_bytes=VMEM_BYTES, collective_id=0, has_side_effects=True),
        name="stack",
    )(mode_scales.reshape(1, keep), plane_counts, links, snapshots, old_modes)
    new_modes, factor = pl.pallas_call(
        functools.partial(factor_kernel, 1.0 / (peers * cells)),
        out_shape=(jax.ShapeDtypeStruct((order, planes, rows_y, rows_z), jnp.bfloat16),
                   jax.ShapeDtypeStruct((order, order), jnp.float32)),
        in_specs=[vmem, vmem, hbm],
        out_specs=(hbm, vmem),
        scratch_shapes=[pltpu.VMEM((order, cells), jnp.bfloat16),
                        pltpu.VMEM((order, order), jnp.float32),
                        pltpu.VMEM((order, order), jnp.float32),
                        pltpu.VMEM((order * rows_y, rows_z), jnp.float32),
                        pltpu.VMEM((planes, order, rows_y, rows_z), jnp.bfloat16),
                        pltpu.SemaphoreType.DMA((1 + planes,))],
        compiler_params=pltpu.CompilerParams(vmem_limit_bytes=VMEM_BYTES),
        name="factor",
    )(gram_new, gram_old, stacked)
    return (new_modes, factor)


def solution(mesh):
    return jax.shard_map(
        shards,
        mesh=mesh,
        in_specs=(
            P(None, ("groups", "blk"), None, None),
            P(None, ("groups", "blk"), None, None),
            P("groups"),
            P(("groups", "blk")),
            P(("groups", "blk"), None),
        ),
        out_specs=(P(None, ("groups", "blk"), None, None), P("groups", None)),
        check_vma=False,
    )
```
